512 devices in a mesh: seq: 32 (over z, x_hi, core), head: 16 (over y, x_lo).
Axes of the slice: x: 4 (x_hi: 2, x_lo: 2; x = x_hi * 2 + x_lo), y: 8, z: 8, core: 2. Of those that a mesh axis runs over, the one named last changes fastest.
Arguments:
- video_qkv: bfloat16 [65536, 3, 2048], P(('seq', 'head')), may hold values from -6 to 6
- audio_qkv: bfloat16 [8192, 3, 2048], P(('seq', 'head')), may hold values from -6 to 6
- pairs: int32 [32, 3], replicated, may hold values from 0 to 1, as said below
Outputs:
- video_out: bfloat16 [65536, 2048], P(('seq', 'head'))
- audio_out: bfloat16 [8192, 2048], P(('seq', 'head'))
The draws below stay inside these ranges and needn't reach their ends.
Inputs may be any that keep to these rules, and one draw needn't show every extreme that they name: pairs[i, k] is 1 when video block i is paired with audio block i + k - 1; the middle column is always 1, and no pair names a block outside the 32 blocks.
All inputs are finite; a program needn't handle non-finite values.
Results may differ from the reference program's by a relative error of at most 0.009.
Values may be sent and summed in bfloat16 or wider, within the bound.
No kernel may reach another device: no remote copies, remote signals or barrier semaphores. Data moves between devices by JAX's collectives and lax.ppermute only.
A program may use at most 64 MiB of HBM per device.

```python
import jax
import jax.numpy as jnp
from jax import lax

HD = 128
HEADS = 16
NBLK = 32
VB = 2048
AB = 256
VTOK = 65536
ATOK = 8192


def draw_video_qkv(key, part):
    key = jax.random.fold_in(key, 11)
    values = jax.random.truncated_normal(key, -6.0, 6.0, (VTOK, 3, HEADS * HD), jnp.float32)
    return values.astype(jnp.bfloat16)


def draw_audio_qkv(key, part):
    key = jax.random.fold_in(key, 23)
    values = jax.random.truncated_normal(key, -6.0, 6.0, (ATOK, 3, HEADS * HD), jnp.float32)
    return values.astype(jnp.bfloat16)


def draw_pairs(key, part):
    key = jax.random.fold_in(key, 37)
    random_bits = jax.random.randint(key, (NBLK, 3), 0, 2, dtype=jnp.int32)
    index = jnp.arange(NBLK, dtype=jnp.int32)
    left = jnp.where(index == 0, 0, random_bits[:, 0])
    right = jnp.where(index == NBLK - 1, 0, random_bits[:, 2])
    middle = jnp.ones((NBLK,), jnp.int32)
    return jnp.stack([left, middle, right], axis=1).astype(jnp.int32)


def setup_inputs(seed: int = 0) -> dict:
    seeds = jax.random.split(jax.random.key(seed), 4)
    return {
        "video_qkv": draw_video_qkv(jax.random.fold_in(seeds[3], 71), 0),
        "audio_qkv": draw_audio_qkv(jax.random.fold_in(seeds[3], 71), 0),
        "pairs": draw_pairs(jax.random.fold_in(seeds[3], 71), 0),
    }


def attend(queries, keys, values, valid):
    scores = jnp.dot(queries, keys.T, preferred_element_type=jnp.float32) * (HD ** -0.5)
    scores = jnp.where(valid[None, :], scores, -jnp.inf)
    largest = jnp.max(scores, axis=1, keepdims=True)
    weights = jnp.exp(scores - largest)
    total = jnp.sum(weights, axis=1, keepdims=True)
    summed = jnp.dot(weights.astype(jnp.bfloat16), values, preferred_element_type=jnp.float32)
    return (summed / total).astype(jnp.bfloat16)


def reference(video_qkv, audio_qkv, pairs):
    video = video_qkv.reshape(NBLK, VB, 3, HEADS, HD)
    audio = audio_qkv.reshape(NBLK, AB, 3, HEADS, HD)
    zeros_five = ((1, 1), (0, 0), (0, 0), (0, 0), (0, 0))
    video_pad = jnp.pad(video, zeros_five)
    audio_pad = jnp.pad(audio, zeros_five)
    flags = jnp.pad(pairs, ((1, 1), (0, 0)))

    def video_item(index):
        block = index // HEADS
        head = index % HEADS
        own = video[block][:, :, head]
        near = lax.dynamic_slice_in_dim(audio_pad, block, 3, 0)[:, :, :, head].reshape(3 * AB, 3, HD)
        keys = jnp.concatenate([own[:, 1], near[:, 1]], axis=0)
        values = jnp.concatenate([own[:, 2], near[:, 2]], axis=0)
        row = lax.dynamic_index_in_dim(flags, block + 1, 0, keepdims=False)
        valid = jnp.concatenate([jnp.ones((VB,), bool), jnp.repeat(row == 1, AB)])
        return attend(own[:, 0], keys, values, valid)

    def audio_item(index):
        block = index // HEADS
        head = index % HEADS
        own = audio[block][:, :, head]
        near = lax.dynamic_slice_in_dim(video_pad, block, 3, 0)[:, :, :, head].reshape(3 * VB, 3, HD)
        keys = jnp.concatenate([own[:, 1], near[:, 1]], axis=0)
        values = jnp.concatenate([own[:, 2], near[:, 2]], axis=0)
        window = lax.dynamic_slice_in_dim(flags, block, 3, 0)
        incoming = jnp.stack([window[0, 2], window[1, 1], window[2, 0]]) == 1
        valid = jnp.concatenate([jnp.ones((AB,), bool), jnp.repeat(incoming, VB)])
        return attend(own[:, 0], keys, values, valid)

    items = jnp.arange(NBLK * HEADS, dtype=jnp.int32)
    video_out = lax.map(video_item, items)
    video_out = video_out.reshape(NBLK, HEADS, VB, HD).transpose(0, 2, 1, 3).reshape(NBLK * VB, HEADS * HD)
    audio_out = lax.map(audio_item, items)
    audio_out = audio_out.reshape(NBLK, HEADS, AB, HD).transpose(0, 2, 1, 3).reshape(NBLK * AB, HEADS * HD)
    return video_out, audio_out
```

```python
import math

import jax
import jax.numpy as jnp
from jax import lax
from jax.experimental import pallas as pl
from jax.experimental.pallas import tpu as pltpu
from jax.sharding import PartitionSpec as P

HD = 128
PEERS = 16
BLOCKS = 32
VT, AT = 128, 16
VB, AB = PEERS * VT, PEERS * AT
KEYS = VB + 3 * AB
STEP = 256
SCALE = math.log2(math.e) / math.sqrt(HD)
VMEM_LIMIT = 48 << 20
BF16, F32 = jnp.bfloat16, jnp.float32
ON_ROWS = (((1,), (1,)), ((), ()))


def rows(ref, part, low, high):
    return ref[:, part, low:high].reshape(PEERS * (high - low), HD)


def stage(place, sources, keys, values):
    for low, (ref, first, last) in zip(place, sources):
        part = ref[:, 1, first:last].reshape(-1, HD)
        keys[low : low + part.shape[0]] = part
        values[low : low + part.shape[0], 0:HD] = ref[:, 2, first:last].reshape(-1, HD)
    values[:, HD : 2 * HD] = jnp.ones((values.shape[0], HD), BF16)


def score(queries, keys, buffer, columns, bias):
    largest = None
    for place, j in enumerate(columns):
        part = lax.dot_general(
            queries, keys[j * STEP : (j + 1) * STEP], ON_ROWS, preferred_element_type=F32
        )
        if j in bias:
            part = part + bias[j]
        buffer[:, place * STEP : (place + 1) * STEP] = part
        for t in range(0, STEP, HD):
            lanes = part[:, t : t + HD]
            largest = lanes if largest is None else jnp.maximum(largest, lanes)
    return jnp.max(largest, axis=1, keepdims=True) * SCALE


def weigh(buffer, columns, largest, values):
    low, high = columns[0] * STEP, (columns[-1] + 1) * STEP
    scores = buffer[:, 0 : high - low]
    weights = jnp.exp2(scores * SCALE - largest).astype(BF16)
    summed = jnp.dot(weights, values[low:high], preferred_element_type=F32)
    return summed[:, :HD], summed[:, HD:]


def pipelined(jobs, buffers, keys, values):
    pending = None
    for index, (load, columns, bias, finish) in enumerate(jobs):
        buffer = buffers.at[index % 2]
        largest = score(load(), keys, buffer, columns, bias)
        if pending is not None:
            pending()

        def pending(buffer=buffer, columns=columns, largest=largest, finish=finish):
            summed, total = weigh(buffer, columns, largest, values)
            finish(summed, total, largest)

    pending()


def pack_kernel(video, audio, out):
    for h in range(PEERS):
        out[h, :, 0:VT] = video[:, :, h * HD : (h + 1) * HD]
        out[h, :, VT:] = audio[:, :, h * HD : (h + 1) * HD]


def unpack_kernel(heads, video, audio):
    for h in range(PEERS):
        video[:, h * HD : (h + 1) * HD] = heads[h, 0:VT]
        audio[:, h * HD : (h + 1) * HD] = heads[h, VT:]


def lend_kernel(own, left, right, to_left, to_right, keys, values, buffers):
    stage((0,), ((own, 0, VT),), keys, values)
    lane = lax.broadcasted_iota(jnp.int32, (AB, HD), 1)

    def job(source, out):
        def finish(summed, total, largest):
            out[0] = (summed / total).astype(BF16)
            level = largest + jnp.log2(total)
            high = level.astype(BF16)
            rest = level - high.astype(F32)
            middle = rest.astype(BF16)
            low = (rest - middle.astype(F32)).astype(BF16)
            out[1] = jnp.where(
                lane < 32, high.astype(F32), jnp.where(lane < 64, middle.astype(F32), low.astype(F32))
            ).astype(BF16)

        return (lambda: rows(source, 0, 0, AT), tuple(range(VB // STEP)), {}, finish)

    pipelined([job(left, to_left), job(right, to_right)], buffers, keys, values)


def main_kernel(pairs, own, left, right, out, audio, level, keys, values, buffers):
    place = lax.axis_index("seq")
    stage(
        (0, VB, VB + AB, VB + 2 * AB),
        ((own, 0, VT), (own, VT, VT + AT), (left, 0, AT), (right, 0, AT)),
        keys,
        values,
    )
    first = VB // STEP + 1
    bias = {
        first: jnp.where(pairs[place, 0] == 1, 0.0, -jnp.inf).astype(F32),
        first + 1: jnp.where(pairs[place, 2] == 1, 0.0, -jnp.inf).astype(F32),
    }
    count = STEP // VT

    def video_job(i):
        def finish(summed, total, largest):
            result = (summed / total).astype(BF16)
            out[i * count : (i + 1) * count, 0:VT] = result.reshape(count, VT, HD)

        return (
            lambda: own[i * count : (i + 1) * count, 0, 0:VT].reshape(STEP, HD),
            tuple(range(KEYS // STEP)),
            bias,
            finish,
        )

    def audio_finish(summed, total, largest):
        audio[...] = summed / total
        level[...] = largest + jnp.log2(total)

    audio_job = (
        lambda: rows(own, 0, VT, VT + AT),
        tuple(range(VB // STEP + 1)),
        {},
        audio_finish,
    )
    pipelined(
        [audio_job] + [video_job(i) for i in range(VB // STEP)], buffers, keys, values
    )


def merge_kernel(pairs, audio, level, from_left, from_right, unused, out):
    place = lax.axis_index("seq")
    left = (place > 0) & (pairs[jnp.maximum(place - 1, 0), 2] == 1)
    right = (place < BLOCKS - 1) & (pairs[jnp.minimum(place + 1, BLOCKS - 1), 0] == 1)

    def level_of(ref, valid):
        split = ref[1].astype(F32)
        value = split[:, 0:1] + split[:, 32:33] + split[:, 64:65]
        return value + jnp.where(valid, 0.0, -jnp.inf).astype(F32)

    levels = [level[:, 0:1], level_of(from_left, left), level_of(from_right, right)]
    largest = jnp.maximum(jnp.maximum(levels[0], levels[1]), levels[2])
    shares = [jnp.exp2(l - largest) for l in levels]
    summed = (
        shares[0] * audio[...]
        + shares[1] * from_left[0].astype(F32)
        + shares[2] * from_right[0].astype(F32)
    )
    result = summed / (shares[0] + shares[1] + shares[2])
    out[...] = result.astype(BF16).reshape(PEERS, AT, HD)


IN_VMEM = pl.BlockSpec(memory_space=pltpu.VMEM)
IN_SMEM = pl.BlockSpec(memory_space=pltpu.SMEM)


def cost(rows_, keys_, moved):
    return pl.CostEstimate(
        flops=4 * rows_ * keys_ * HD, bytes_accessed=moved, transcendentals=rows_ * keys_
    )


def scratch(keys_):
    return [
        pltpu.VMEM((keys_, HD), BF16),
        pltpu.VMEM((keys_, 2 * HD), BF16),
        pltpu.VMEM((2, STEP, keys_), F32),
    ]


def on_device(video_qkv, audio_qkv, pairs):
    params = pltpu.CompilerParams(vmem_limit_bytes=VMEM_LIMIT)
    tokens = pl.pallas_call(
        pack_kernel,
        out_shape=jax.ShapeDtypeStruct((PEERS, 3, VT + AT, HD), BF16),
        in_specs=[IN_VMEM] * 2,
        out_specs=IN_VMEM,
        compiler_params=params,
        name="pack",
    )(video_qkv.transpose(1, 0, 2), audio_qkv.transpose(1, 0, 2))
    own = lax.all_to_all(tokens, "head", split_axis=0, concat_axis=0, tiled=True)
    forward = [(i, i + 1) for i in range(BLOCKS - 1)]
    backward = [(i + 1, i) for i in range(BLOCKS - 1)]
    own_audio = own[:, :, VT:]
    left = lax.ppermute(own_audio, "seq", forward)
    right = lax.ppermute(own_audio, "seq", backward)
    part = jax.ShapeDtypeStruct((2, AB, HD), BF16)
    to_left, to_right = pl.pallas_call(
        lend_kernel,
        out_shape=(part, part),
        in_specs=[IN_VMEM] * 3,
        out_specs=(IN_VMEM, IN_VMEM),
        scratch_shapes=scratch(VB),
        compiler_params=params,
        cost_estimate=cost(2 * AB, VB, 2 << 20),
        name="lend",
    )(own, left, right)
    from_left = lax.ppermute(to_right, "seq", forward)
    from_right = lax.ppermute(to_left, "seq", backward)
    packed = jax.ShapeDtypeStruct((PEERS, VT + AT, HD), BF16)
    single = jax.ShapeDtypeStruct((AB, HD), F32)
    out, audio, level = pl.pallas_call(
        main_kernel,
        out_shape=(packed, single, single),
        in_specs=[IN_SMEM] + [IN_VMEM] * 3,
        out_specs=(IN_VMEM,) * 3,
        scratch_shapes=scratch(KEYS),
        compiler_params=params,
        cost_estimate=cost(VB + AB, KEYS, 3 << 20),
        name="attend",
    )(pairs, own, left, right)
    rows_of_audio = pl.BlockSpec((PEERS, AT, HD), lambda i: (0, VT // AT, 0))
    out = pl.pallas_call(
        merge_kernel,
        out_shape=packed,
        grid=(1,),
        in_specs=[IN_SMEM] + [IN_VMEM] * 4 + [pl.BlockSpec(memory_space=pl.ANY)],
        out_specs=rows_of_audio,
        input_output_aliases={5: 0},
        compiler_params=params,
        name="merge",
    )(pairs, audio, level, from_left, from_right, out)
    back = lax.all_to_all(out, "head", split_axis=0, concat_axis=0, tiled=True)
    return pl.pallas_call(
        unpack_kernel,
        out_shape=(
            jax.ShapeDtypeStruct((VT, PEERS * HD), BF16),
            jax.ShapeDtypeStruct((AT, PEERS * HD), BF16),
        ),
        in_specs=[IN_VMEM],
        out_specs=(IN_VMEM, IN_VMEM),
        compiler_params=params,
        name="unpack",
    )(back)


def solution(mesh):
    return jax.shard_map(
        on_device,
        mesh=mesh,
        in_specs=(P(("seq", "head"), None, None), P(("seq", "head"), None, None), P()),
        out_specs=(P(("seq", "head"), None), P(("seq", "head"), None)),
        check_vma=False,
    )
```

```python
import math

import jax
import jax.numpy as jnp
from jax import lax
from jax.experimental import pallas as pl
from jax.experimental.pallas import tpu as pltpu
from jax.sharding import PartitionSpec as P

HD = 128
PEERS = 16
BLOCKS = 32
VT, AT = 128, 16
VB, AB = PEERS * VT, PEERS * AT
KEYS = VB + 3 * AB
STEP = 256
SCALE = math.log2(math.e) / math.sqrt(HD)
VMEM_LIMIT = 32 << 20
PACK_LIMIT = 59 << 20
BF16, F32 = jnp.bfloat16, jnp.float32
ON_ROWS = (((1,), (1,)), ((), ()))


VIDEO_Q, VIDEO_K, VIDEO_V = ((c * VT, (c + 1) * VT) for c in range(3))
AUDIO_Q, AUDIO_K, AUDIO_V = ((c * AT, (c + 1) * AT) for c in range(3))


def rows(ref, span):
    return ref[:, span[0] : span[1]].reshape(-1, HD)


def stage(sources, keys, values):
    low = 0
    for ref, key_span, value_span in sources:
        part = rows(ref, key_span)
        keys[low : low + part.shape[0]] = part
        values[low : low + part.shape[0], 0:HD] = rows(ref, value_span)
        low += part.shape[0]
    values[:, HD : 2 * HD] = jnp.ones((values.shape[0], HD), BF16)


def score(queries, keys, buffer, columns, bias):
    largest = None
    for place, j in enumerate(columns):
        part = lax.dot_general(
            queries, keys[j * STEP : (j + 1) * STEP], ON_ROWS, preferred_element_type=F32
        )
        if j in bias:
            part = part + bias[j]
        buffer[:, place * STEP : (place + 1) * STEP] = part
        for t in range(0, STEP, HD):
            lanes = part[:, t : t + HD]
            largest = lanes if largest is None else jnp.maximum(largest, lanes)
    return jnp.max(largest, axis=1, keepdims=True) * SCALE


def weigh(buffer, columns, largest, values):
    low, high = columns[0] * STEP, (columns[-1] + 1) * STEP
    scores = buffer[:, 0 : high - low]
    weights = jnp.exp2(scores * SCALE - largest).astype(BF16)
    summed = jnp.dot(weights, values[low:high], preferred_element_type=F32)
    return summed[:, :HD], summed[:, HD:]


def pipelined(jobs, buffers, keys, values):
    pending = None
    for index, (load, columns, bias, finish) in enumerate(jobs):
        buffer = buffers.at[index % 2]
        largest = score(load(), keys, buffer, columns, bias)
        if pending is not None:
            pending()

        def pending(buffer=buffer, columns=columns, largest=largest, finish=finish):
            summed, total = weigh(buffer, columns, largest, values)
            finish(summed, total, largest)

    pending()


def pack_kernel(source, out, held, sems):
    cuts, _, count, _ = held.shape
    tokens = cuts * count
    copies = [
        pltpu.make_async_copy(source.at[:, i * count : (i + 1) * count], held.at[i], sems.at[i])
        for i in range(cuts)
    ]
    for copy in copies:
        copy.start()
    for i in range(cuts):
        copies[i].wait()
        for h in range(PEERS):
            for c in range(3):
                low = c * tokens + i * count
                out[h, low : low + count] = held[i, c, :, h * HD : (h + 1) * HD]


FAR_AT, MARKS_AT, NEAR_AT, OWN_AT = range(4)
FAR, NEAR, OWN = range(3)


def unpack_kernel(heads, video):
    for h in range(PEERS):
        video[:, h * HD : (h + 1) * HD] = heads[h]


def pieces(level):
    high = level.astype(BF16).astype(F32)
    middle = (level - high).astype(BF16).astype(F32)
    return high, middle, level - high - middle


def lend_kernel(own, audio, far, near, parts, keys, values, buffers, levels):
    stage([(own, VIDEO_K, VIDEO_V), (audio, AUDIO_K, AUDIO_V)], keys, values)

    def job(source, count, slot, at):
        def finish(summed, total, largest):
            parts[:, at] = (summed / total).astype(BF16).reshape(PEERS, AT, HD)
            levels[slot] = largest + jnp.log2(total)

        return (lambda: rows(source, AUDIO_Q), tuple(range(count // STEP)), {}, finish)

    jobs = [
        job(audio, VB + AB, OWN, OWN_AT),
        job(near, VB, NEAR, NEAR_AT),
        job(far, VB, FAR, FAR_AT),
    ]
    pipelined(jobs, buffers, keys, values)
    lane = lax.broadcasted_iota(jnp.int32, (AB, HD), 1)
    marks = jnp.zeros((AB, HD), F32)
    for slot in (FAR, NEAR, OWN):
        for k, piece in enumerate(pieces(levels[slot])):
            marks = jnp.where(lane == 3 * slot + k, piece, marks)
    parts[:, MARKS_AT] = marks.astype(BF16).reshape(PEERS, AT, HD)


def main_kernel(pairs, own, audio, far, near, out, keys, values, buffers):
    place = lax.axis_index("seq")
    stage([(own, VIDEO_K, VIDEO_V)] + [(a, AUDIO_K, AUDIO_V) for a in (audio, far, near)], keys, values)
    even = lax.rem(place, 2) == 0
    left, right = pairs[place, 0] == 1, pairs[place, 2] == 1
    far_valid, near_valid = jnp.where(even, left, right), jnp.where(even, right, left)
    first = VB // STEP + 1
    bias = {
        first: jnp.where(far_valid, 0.0, -jnp.inf).astype(F32),
        first + 1: jnp.where(near_valid, 0.0, -jnp.inf).astype(F32),
    }
    count = STEP // VT

    def job(i):
        low, high = i * count, (i + 1) * count

        def finish(summed, total, largest):
            result = (summed / total).astype(BF16)
            out[low:high] = result.reshape(count, VT, HD)

        def load():
            return own[low:high, 0:VT].reshape(STEP, HD)

        return (load, tuple(range(KEYS // STEP)), bias, finish)

    pipelined([job(i) for i in range(VB // STEP)], buffers, keys, values)


def merge_kernel(pairs, parts, from_far, from_near, out):
    place = lax.axis_index("seq")
    left = (place > 0) & (pairs[jnp.maximum(place - 1, 0), 2] == 1)
    right = (place < BLOCKS - 1) & (pairs[jnp.minimum(place + 1, BLOCKS - 1), 0] == 1)
    even = lax.rem(place, 2) == 0
    far_valid, near_valid = jnp.where(even, left, right), jnp.where(even, right, left)

    def level(marks, slot):
        marks = marks.astype(F32).reshape(AB, HD)
        return sum(marks[:, 3 * slot + k : 3 * slot + k + 1] for k in range(3))

    def masked(value, valid):
        return value + jnp.where(valid, 0.0, -jnp.inf).astype(F32)

    levels = [
        level(parts[:, MARKS_AT], OWN),
        masked(level(from_far[:, 1], FAR), far_valid),
        masked(level(from_near[:, 0], NEAR), near_valid),
    ]
    largest = jnp.maximum(jnp.maximum(levels[0], levels[1]), levels[2])
    shares = [jnp.exp2(l - largest) for l in levels]
    summed = jnp.zeros((AB, HD), F32)
    for share, part in zip(shares, (parts[:, OWN_AT], from_far[:, 0], from_near[:, 1])):
        summed = summed + share * part.astype(F32).reshape(AB, HD)
    result = (summed / (shares[0] + shares[1] + shares[2])).astype(BF16)
    for h in range(PEERS):
        out[:, h * HD : (h + 1) * HD] = result[h * AT : (h + 1) * AT]


IN_VMEM = pl.BlockSpec(memory_space=pltpu.VMEM)
IN_PLACE = pl.BlockSpec(memory_space=pltpu.HBM)
IN_SMEM = pl.BlockSpec(memory_space=pltpu.SMEM)


def cost(rows_, keys_, moved):
    return pl.CostEstimate(
        flops=4 * rows_ * keys_ * HD, bytes_accessed=moved, transcendentals=rows_ * keys_
    )


def scratch(keys_):
    return [
        pltpu.VMEM((keys_, HD), BF16),
        pltpu.VMEM((keys_, 2 * HD), BF16),
        pltpu.VMEM((2, STEP, keys_), F32),
    ]


def swap(block, first):
    pairs_ = [(i, i + 1) for i in range(first, BLOCKS - 1, 2)]
    return lax.ppermute(block, "seq", pairs_ + [(j, i) for i, j in pairs_])


def on_device(video_qkv, audio_qkv, pairs):
    params = pltpu.CompilerParams(vmem_limit_bytes=VMEM_LIMIT)
    video, audio = video_qkv.transpose(1, 0, 2), audio_qkv.transpose(1, 0, 2)

    def sent(source, tokens, cuts, name):
        return pl.pallas_call(
            pack_kernel,
            out_shape=jax.ShapeDtypeStruct((PEERS, 3 * tokens, HD), BF16),
            in_specs=[IN_PLACE],
            out_specs=IN_VMEM,
            scratch_shapes=[
                pltpu.VMEM((cuts, 3, tokens // cuts, PEERS * HD), BF16),
                pltpu.SemaphoreType.DMA((cuts,)),
            ],
            compiler_params=pltpu.CompilerParams(vmem_limit_bytes=PACK_LIMIT),
            cost_estimate=pl.CostEstimate(
                flops=0, bytes_accessed=tokens * 3 * PEERS * HD * 4, transcendentals=0
            ),
            name=name,
        )(source)

    def exchanged(block):
        return lax.all_to_all(block, "head", split_axis=0, concat_axis=0, tiled=True)

    own_audio = exchanged(sent(audio, AT, 1, "pack_audio"))
    own = exchanged(sent(video, VT, 4, "pack_video"))
    far = swap(own_audio, 1)
    near = swap(own_audio, 0)
    parts = pl.pallas_call(
        lend_kernel,
        out_shape=jax.ShapeDtypeStruct((PEERS, 4, AT, HD), BF16),
        in_specs=[IN_VMEM] * 4,
        out_specs=IN_VMEM,
        scratch_shapes=scratch(VB + AB) + [pltpu.VMEM((3, AB, HD), F32)],
        compiler_params=params,
        cost_estimate=cost(3 * AB, VB, 2 << 20),
        name="lend",
    )(own, own_audio, far, near)
    parts = exchanged(parts)
    out = pl.pallas_call(
        main_kernel,
        out_shape=jax.ShapeDtypeStruct((PEERS, VT, HD), BF16),
        in_specs=[IN_SMEM] + [IN_VMEM] * 4,
        out_specs=IN_VMEM,
        scratch_shapes=scratch(KEYS),
        compiler_params=params,
        cost_estimate=cost(VB, KEYS, 3 << 20),
        name="attend",
    )(pairs, own, own_audio, far, near)
    back = exchanged(out)
    from_far = swap(parts[:, FAR_AT : MARKS_AT + 1], 1)
    from_near = swap(parts[:, MARKS_AT : NEAR_AT + 1], 0)
    audio_out = pl.pallas_call(
        merge_kernel,
        out_shape=jax.ShapeDtypeStruct((AT, PEERS * HD), BF16),
        in_specs=[IN_SMEM] + [IN_VMEM] * 3,
        out_specs=IN_VMEM,
        compiler_params=params,
        name="merge",
    )(pairs, parts, from_far, from_near)
    video_out = pl.pallas_call(
        unpack_kernel,
        out_shape=jax.ShapeDtypeStruct((VT, PEERS * HD), BF16),
        in_specs=[IN_VMEM],
        out_specs=IN_VMEM,
        compiler_params=params,
        name="unpack",
    )(back)
    return video_out, audio_out


def solution(mesh):
    return jax.shard_map(
        on_device,
        mesh=mesh,
        in_specs=(P(("seq", "head"), None, None), P(("seq", "head"), None, None), P()),
        out_specs=(P(("seq", "head"), None), P(("seq", "head"), None)),
        check_vma=False,
    )
```

```python
import math

import jax
import jax.numpy as jnp
from jax import lax
from jax.experimental import pallas as pl
from jax.experimental.pallas import tpu as pltpu
from jax.sharding import PartitionSpec as P

HD = 128
PEERS = 16
BLOCKS = 32
VT, AT = 128, 16
VB, AB = PEERS * VT, PEERS * AT
KEYS = VB + 3 * AB
STEP = 256
SCALE = math.log2(math.e) / math.sqrt(HD)
VMEM_LIMIT = 32 << 20
PACK_LIMIT = 59 << 20
BF16, F32 = jnp.bfloat16, jnp.float32
ON_ROWS = (((1,), (1,)), ((), ()))


VIDEO_Q, VIDEO_K, VIDEO_V = ((c * VT, (c + 1) * VT) for c in range(3))
AUDIO_Q, AUDIO_K, AUDIO_V = ((c * AT, (c + 1) * AT) for c in range(3))


def rows(ref, span):
    return ref[:, span[0] : span[1]].reshape(-1, HD)


def stage(sources, keys, values):
    low = 0
    for ref, key_span, value_span in sources:
        part = rows(ref, key_span)
        keys[low : low + part.shape[0]] = part
        values[low : low + part.shape[0], 0:HD] = rows(ref, value_span)
        low += part.shape[0]
    values[:, HD : 2 * HD] = jnp.ones((values.shape[0], HD), BF16)


def score(queries, keys, buffer, columns, bias):
    largest = None
    for place, j in enumerate(columns):
        part = lax.dot_general(
            queries, keys[j * STEP : (j + 1) * STEP], ON_ROWS, preferred_element_type=F32
        )
        if j in bias:
            part = part + bias[j]
        buffer[:, place * STEP : (place + 1) * STEP] = part
        for t in range(0, STEP, HD):
            lanes = part[:, t : t + HD]
            largest = lanes if largest is None else jnp.maximum(largest, lanes)
    return jnp.max(largest, axis=1, keepdims=True) * SCALE


def weigh(buffer, columns, largest, values):
    low, high = columns[0] * STEP, (columns[-1] + 1) * STEP
    scores = buffer[:, 0 : high - low]
    weights = jnp.exp2(scores * SCALE - largest).astype(BF16)
    summed = jnp.dot(weights, values[low:high], preferred_element_type=F32)
    return summed[:, :HD], summed[:, HD:]


def pipelined(jobs, buffers, keys, values):
    pending = None
    for index, (load, columns, bias, finish) in enumerate(jobs):
        buffer = buffers.at[index % 2]
        largest = score(load(), keys, buffer, columns, bias)
        if pending is not None:
            pending()

        def pending(buffer=buffer, columns=columns, largest=largest, finish=finish):
            summed, total = weigh(buffer, columns, largest, values)
            finish(summed, total, largest)

    pending()


def pack_kernel(source, out, held, sems):
    cuts, _, count, _ = held.shape
    tokens = cuts * count
    copies = [
        pltpu.make_async_copy(source.at[:, i * count : (i + 1) * count], held.at[i], sems.at[i])
        for i in range(cuts)
    ]
    for copy in copies:
        copy.start()
    for i in range(cuts):
        copies[i].wait()
        for h in range(PEERS):
            for c in range(3):
                low = c * tokens + i * count
                out[h, low : low + count] = held[i, c, :, h * HD : (h + 1) * HD]


FAR_AT, MARKS_AT, NEAR_AT, OWN_AT = range(4)
FAR, NEAR, OWN = range(3)


def unpack_kernel(heads, video, held, sems):
    cuts, count, _ = held.shape
    copies = [
        pltpu.make_async_copy(held.at[i], video.at[i * count : (i + 1) * count], sems.at[i])
        for i in range(cuts)
    ]
    for i in range(cuts):
        for h in range(PEERS):
            held[i, :, h * HD : (h + 1) * HD] = heads[h, i * count : (i + 1) * count]
        copies[i].start()
    for copy in copies:
        copy.wait()


def pieces(level):
    high = level.astype(BF16).astype(F32)
    middle = (level - high).astype(BF16).astype(F32)
    return high, middle, level - high - middle


def lend_kernel(own, audio, far, near, out, keys, values, buffers, levels, parts, sems):
    stage([(own, VIDEO_K, VIDEO_V), (audio, AUDIO_K, AUDIO_V)], keys, values)
    copies = [pltpu.make_async_copy(parts.at[i], out.at[:, i], sems.at[i]) for i in range(4)]

    def job(source, count, slot, at):
        def finish(summed, total, largest):
            parts[at] = (summed / total).astype(BF16).reshape(PEERS, AT, HD)
            copies[at].start()
            levels[slot] = largest + jnp.log2(total)

        return (lambda: rows(source, AUDIO_Q), tuple(range(count // STEP)), {}, finish)

    jobs = [
        job(audio, VB + AB, OWN, OWN_AT),
        job(near, VB, NEAR, NEAR_AT),
        job(far, VB, FAR, FAR_AT),
    ]
    pipelined(jobs, buffers, keys, values)
    lane = lax.broadcasted_iota(jnp.int32, (AB, HD), 1)
    marks = jnp.zeros((AB, HD), F32)
    for slot in (FAR, NEAR, OWN):
        for k, piece in enumerate(pieces(levels[slot])):
            marks = jnp.where(lane == 3 * slot + k, piece, marks)
    parts[MARKS_AT] = marks.astype(BF16).reshape(PEERS, AT, HD)
    copies[MARKS_AT].start()
    for copy in copies:
        copy.wait()


def main_kernel(pairs, own, audio, far, near, out, keys, values, buffers, held, sems):
    place = lax.axis_index("seq")
    stage([(own, VIDEO_K, VIDEO_V)] + [(a, AUDIO_K, AUDIO_V) for a in (audio, far, near)], keys, values)
    even = lax.rem(place, 2) == 0
    left, right = pairs[place, 0] == 1, pairs[place, 2] == 1
    far_valid, near_valid = jnp.where(even, left, right), jnp.where(even, right, left)
    first = VB // STEP + 1
    bias = {
        first: jnp.where(far_valid, 0.0, -jnp.inf).astype(F32),
        first + 1: jnp.where(near_valid, 0.0, -jnp.inf).astype(F32),
    }
    count = STEP // VT

    def job(i):
        low, high = i * count, (i + 1) * count

        def finish(summed, total, largest):
            held[low:high] = (summed / total).astype(BF16).reshape(count, VT, HD)
            copies[i].start()

        def load():
            return own[low:high, 0:VT].reshape(STEP, HD)

        return (load, tuple(range(KEYS // STEP)), bias, finish)

    steps = range(VB // STEP)
    copies = [
        pltpu.make_async_copy(
            held.at[i * count : (i + 1) * count], out.at[i * count : (i + 1) * count], sems.at[i]
        )
        for i in steps
    ]
    pipelined([job(i) for i in steps], buffers, keys, values)
    for copy in copies:
        copy.wait()


def merge_kernel(pairs, parts, from_far, from_near, out):
    place = lax.axis_index("seq")
    left = (place > 0) & (pairs[jnp.maximum(place - 1, 0), 2] == 1)
    right = (place < BLOCKS - 1) & (pairs[jnp.minimum(place + 1, BLOCKS - 1), 0] == 1)
    even = lax.rem(place, 2) == 0
    far_valid, near_valid = jnp.where(even, left, right), jnp.where(even, right, left)

    row = lax.broadcasted_iota(jnp.int32, (HD, HD), 0)

    def level(marks, slot):
        wanted = (row >= 3 * slot) & (row < 3 * slot + 3)
        chosen = jnp.where(wanted, 1.0, 0.0).astype(BF16)
        return jnp.dot(marks.reshape(AB, HD), chosen, preferred_element_type=F32)

    def masked(value, valid):
        return value + jnp.where(valid, 0.0, -jnp.inf).astype(F32)

    levels = [
        level(parts[:, MARKS_AT], OWN),
        masked(level(from_far[:, 1], FAR), far_valid),
        masked(level(from_near[:, 0], NEAR), near_valid),
    ]
    largest = jnp.maximum(jnp.maximum(levels[0], levels[1]), levels[2])
    shares = [jnp.exp2(l - largest) for l in levels]
    summed = jnp.zeros((AB, HD), F32)
    for share, part in zip(shares, (parts[:, OWN_AT], from_far[:, 0], from_near[:, 1])):
        summed = summed + share * part.astype(F32).reshape(AB, HD)
    result = (summed / (shares[0] + shares[1] + shares[2])).astype(BF16)
    for h in range(PEERS):
        out[:, h * HD : (h + 1) * HD] = result[h * AT : (h + 1) * AT]


IN_VMEM = pl.BlockSpec(memory_space=pltpu.VMEM)
IN_PLACE = pl.BlockSpec(memory_space=pltpu.HBM)
IN_SMEM = pl.BlockSpec(memory_space=pltpu.SMEM)


def cost(rows_, keys_, moved):
    return pl.CostEstimate(
        flops=4 * rows_ * keys_ * HD, bytes_accessed=moved, transcendentals=rows_ * keys_
    )


def scratch(keys_):
    return [
        pltpu.VMEM((keys_, HD), BF16),
        pltpu.VMEM((keys_, 2 * HD), BF16),
        pltpu.VMEM((2, STEP, keys_), F32),
    ]


def swap(block, first):
    pairs_ = [(i, i + 1) for i in range(first, BLOCKS - 1, 2)]
    return lax.ppermute(block, "seq", pairs_ + [(j, i) for i, j in pairs_])


def on_device(video_qkv, audio_qkv, pairs):
    params = pltpu.CompilerParams(vmem_limit_bytes=VMEM_LIMIT)
    pack_params = pltpu.CompilerParams(vmem_limit_bytes=PACK_LIMIT)

    cuts = 4
    packed_video = pl.pallas_call(
        pack_kernel,
        out_shape=jax.ShapeDtypeStruct((PEERS, 3 * VT, HD), BF16),
        in_specs=[IN_PLACE],
        out_specs=IN_VMEM,
        scratch_shapes=[
            pltpu.VMEM((cuts, 3, VT // cuts, PEERS * HD), BF16),
            pltpu.SemaphoreType.DMA((cuts,)),
        ],
        compiler_params=pack_params,
        cost_estimate=pl.CostEstimate(flops=0, bytes_accessed=4 << 20, transcendentals=0),
        name="pack_video",
    )(video_qkv.transpose(1, 0, 2))

    def exchanged(block):
        return lax.all_to_all(block, "head", split_axis=0, concat_axis=0, tiled=True)

    turned = audio_qkv.reshape(AT, 3, PEERS, HD).transpose(2, 1, 0, 3)
    own_audio = exchanged(turned.reshape(PEERS, 3 * AT, HD))
    own = exchanged(packed_video)
    far = swap(own_audio, 1)
    near = swap(own_audio, 0)
    parts = pl.pallas_call(
        lend_kernel,
        out_shape=jax.ShapeDtypeStruct((PEERS, 4, AT, HD), BF16),
        in_specs=[IN_VMEM] * 4,
        out_specs=IN_PLACE,
        scratch_shapes=scratch(VB + AB)
        + [
            pltpu.VMEM((3, AB, HD), F32),
            pltpu.VMEM((4, PEERS, AT, HD), BF16),
            pltpu.SemaphoreType.DMA((4,)),
        ],
        compiler_params=params,
        cost_estimate=cost(3 * AB, VB, 2 << 20),
        name="lend",
    )(own, own_audio, far, near)
    parts = exchanged(parts)
    out = pl.pallas_call(
        main_kernel,
        out_shape=jax.ShapeDtypeStruct((PEERS, VT, HD), BF16),
        in_specs=[IN_SMEM] + [IN_VMEM] * 4,
        out_specs=IN_PLACE,
        scratch_shapes=scratch(KEYS)
        + [pltpu.VMEM((PEERS, VT, HD), BF16), pltpu.SemaphoreType.DMA((VB // STEP,))],
        compiler_params=params,
        cost_estimate=cost(VB, KEYS, 3 << 20),
        name="attend",
    )(pairs, own, own_audio, far, near)
    back = exchanged(out)
    from_far = swap(parts[:, FAR_AT : MARKS_AT + 1], 1)
    from_near = swap(parts[:, MARKS_AT : NEAR_AT + 1], 0)
    audio_out = pl.pallas_call(
        merge_kernel,
        out_shape=jax.ShapeDtypeStruct((AT, PEERS * HD), BF16),
        in_specs=[IN_SMEM] + [IN_VMEM] * 3,
        out_specs=IN_VMEM,
        compiler_params=params,
        name="merge",
    )(pairs, parts, from_far, from_near)
    video_out = pl.pallas_call(
        unpack_kernel,
        out_shape=jax.ShapeDtypeStruct((VT, PEERS * HD), BF16),
        in_specs=[IN_VMEM],
        out_specs=IN_PLACE,
        scratch_shapes=[
            pltpu.VMEM((4, VT // 4, PEERS * HD), BF16),
            pltpu.SemaphoreType.DMA((4,)),
        ],
        compiler_params=params,
        name="unpack",
    )(back)
    return video_out, audio_out


def solution(mesh):
    return jax.shard_map(
        on_device,
        mesh=mesh,
        in_specs=(P(("seq", "head"), None, None), P(("seq", "head"), None, None), P()),
        out_specs=(P(("seq", "head"), None), P(("seq", "head"), None)),
        check_vma=False,
    )
```

```python
import math

import jax
import jax.numpy as jnp
from jax import lax
from jax.experimental import pallas as pl
from jax.experimental.pallas import tpu as pltpu
from jax.sharding import PartitionSpec as P

HD = 128
PEERS = 16
BLOCKS = 32
VT, AT = 128, 16
VB, AB = PEERS * VT, PEERS * AT
KEYS = VB + 3 * AB
STEP = 256
SCALE = math.log2(math.e) / math.sqrt(HD)
VMEM_LIMIT = 32 << 20
PACK_LIMIT = 59 << 20
BF16, F32 = jnp.bfloat16, jnp.float32
ON_ROWS = (((1,), (1,)), ((), ()))


VIDEO_Q, VIDEO_K, VIDEO_V = ((c * VT, (c + 1) * VT) for c in range(3))
AUDIO_Q, AUDIO_K, AUDIO_V = ((c * AT, (c + 1) * AT) for c in range(3))


def rows(ref, span):
    return ref[:, span[0] : span[1]].reshape(-1, HD)


def stage(sources, keys, values):
    low = 0
    for ref, key_span, value_span in sources:
        part = rows(ref, value_span)
        values[low : low + part.shape[0], 0:HD] = part
        if low >= VB:
            keys[low - VB : low - VB + part.shape[0]] = rows(ref, key_span)
        low += part.shape[0]
    values[:, HD : 2 * HD] = jnp.ones((values.shape[0], HD), BF16)


def key_step(own, keys, j):
    video = VB // STEP
    if j >= video:
        return keys[(j - video) * STEP : (j - video + 1) * STEP]
    count = STEP // VT
    return own[j * count : (j + 1) * count, VIDEO_K[0] : VIDEO_K[1]].reshape(STEP, HD)


def score(queries, keys, buffer, columns, bias):
    largest = None
    for place, j in enumerate(columns):
        part = lax.dot_general(
            queries, key_step(*keys, j), ON_ROWS, preferred_element_type=F32
        )
        if j in bias:
            part = part + bias[j]
        buffer[:, place * STEP : (place + 1) * STEP] = part
        for t in range(0, STEP, HD):
            lanes = part[:, t : t + HD]
            largest = lanes if largest is None else jnp.maximum(largest, lanes)
    return jnp.max(largest, axis=1, keepdims=True) * SCALE


def weigh(buffer, columns, largest, values):
    low, high = columns[0] * STEP, (columns[-1] + 1) * STEP
    scores = buffer[:, 0 : high - low]
    weights = jnp.exp2(scores * SCALE - largest).astype(BF16)
    summed = jnp.dot(weights, values[low:high], preferred_element_type=F32)
    return summed[:, :HD], summed[:, HD:]


def pipelined(jobs, buffers, keys, values):
    pending = None
    for index, (load, columns, bias, finish) in enumerate(jobs):
        buffer = buffers.at[index % 2]
        largest = score(load(), keys, buffer, columns, bias)
        if pending is not None:
            pending()

        def pending(buffer=buffer, columns=columns, largest=largest, finish=finish):
            summed, total = weigh(buffer, columns, largest, values)
            finish(summed, total, largest)

    pending()


def pack_kernel(source, out, held, sems):
    cuts, _, count, _ = held.shape
    tokens = cuts * count
    copies = [
        pltpu.make_async_copy(source.at[:, i * count : (i + 1) * count], held.at[i], sems.at[i])
        for i in range(cuts)
    ]
    for copy in copies:
        copy.start()
    for i in range(cuts):
        copies[i].wait()
        for h in range(PEERS):
            for c in range(3):
                low = c * tokens + i * count
                out[h, low : low + count] = held[i, c, :, h * HD : (h + 1) * HD]


FAR_AT, MARKS_AT, NEAR_AT, OWN_AT = range(4)
FAR, NEAR, OWN = range(3)


def unpack_kernel(heads, video, held, sems):
    cuts, count, _ = held.shape
    copies = [
        pltpu.make_async_copy(held.at[i], video.at[i * count : (i + 1) * count], sems.at[i])
        for i in range(cuts)
    ]
    for i in range(cuts):
        for h in range(PEERS):
            held[i, :, h * HD : (h + 1) * HD] = heads[h, i * count : (i + 1) * count]
        copies[i].start()
    for copy in copies:
        copy.wait()


def pieces(level):
    high = level.astype(BF16).astype(F32)
    middle = (level - high).astype(BF16).astype(F32)
    return high, middle, level - high - middle


def lend_kernel(own, audio, far, near, out, keys, values, buffers, levels, parts, sems):
    stage([(own, VIDEO_K, VIDEO_V), (audio, AUDIO_K, AUDIO_V)], keys, values)
    copies = [pltpu.make_async_copy(parts.at[i], out.at[:, i], sems.at[i]) for i in range(4)]

    def job(source, count, slot, at):
        def finish(summed, total, largest):
            parts[at] = (summed / total).astype(BF16).reshape(PEERS, AT, HD)
            copies[at].start()
            levels[slot] = largest + jnp.log2(total)

        return (lambda: rows(source, AUDIO_Q), tuple(range(count // STEP)), {}, finish)

    jobs = [
        job(audio, VB + AB, OWN, OWN_AT),
        job(near, VB, NEAR, NEAR_AT),
        job(far, VB, FAR, FAR_AT),
    ]
    pipelined(jobs, buffers, (own, keys), values)
    lane = lax.broadcasted_iota(jnp.int32, (AB, HD), 1)
    marks = jnp.zeros((AB, HD), F32)
    for slot in (FAR, NEAR, OWN):
        for k, piece in enumerate(pieces(levels[slot])):
            marks = jnp.where(lane == 3 * slot + k, piece, marks)
    parts[MARKS_AT] = marks.astype(BF16).reshape(PEERS, AT, HD)
    copies[MARKS_AT].start()
    for copy in copies:
        copy.wait()


def main_kernel(pairs, own, audio, far, near, out, keys, values, buffers, held, sems):
    place = lax.axis_index("seq")
    stage([(own, VIDEO_K, VIDEO_V)] + [(a, AUDIO_K, AUDIO_V) for a in (audio, far, near)], keys, values)
    even = lax.rem(place, 2) == 0
    left, right = pairs[place, 0] == 1, pairs[place, 2] == 1
    far_valid, near_valid = jnp.where(even, left, right), jnp.where(even, right, left)
    first = VB // STEP + 1
    bias = {
        first: jnp.where(far_valid, 0.0, -jnp.inf).astype(F32),
        first + 1: jnp.where(near_valid, 0.0, -jnp.inf).astype(F32),
    }
    count = STEP // VT

    def job(i):
        low, high = i * count, (i + 1) * count

        def finish(summed, total, largest):
            held[low:high] = (summed / total).astype(BF16).reshape(count, VT, HD)
            copies[i].start()

        def load():
            return own[low:high, 0:VT].reshape(STEP, HD)

        return (load, tuple(range(KEYS // STEP)), bias, finish)

    steps = range(VB // STEP)
    copies = [
        pltpu.make_async_copy(
            held.at[i * count : (i + 1) * count], out.at[i * count : (i + 1) * count], sems.at[i]
        )
        for i in steps
    ]
    pipelined([job(i) for i in steps], buffers, (own, keys), values)
    for copy in copies:
        copy.wait()


def merge_kernel(pairs, parts, from_far, from_near, out):
    place = lax.axis_index("seq")
    left = (place > 0) & (pairs[jnp.maximum(place - 1, 0), 2] == 1)
    right = (place < BLOCKS - 1) & (pairs[jnp.minimum(place + 1, BLOCKS - 1), 0] == 1)
    even = lax.rem(place, 2) == 0
    far_valid, near_valid = jnp.where(even, left, right), jnp.where(even, right, left)

    row = lax.broadcasted_iota(jnp.int32, (HD, HD), 0)

    def level(marks, slot):
        wanted = (row >= 3 * slot) & (row < 3 * slot + 3)
        chosen = jnp.where(wanted, 1.0, 0.0).astype(BF16)
        return jnp.dot(marks.reshape(AB, HD), chosen, preferred_element_type=F32)

    def masked(value, valid):
        return value + jnp.where(valid, 0.0, -jnp.inf).astype(F32)

    levels = [
        level(parts[:, MARKS_AT], OWN),
        masked(level(from_far[:, 1], FAR), far_valid),
        masked(level(from_near[:, 0], NEAR), near_valid),
    ]
    largest = jnp.maximum(jnp.maximum(levels[0], levels[1]), levels[2])
    shares = [jnp.exp2(l - largest) for l in levels]
    summed = jnp.zeros((AB, HD), F32)
    for share, part in zip(shares, (parts[:, OWN_AT], from_far[:, 0], from_near[:, 1])):
        summed = summed + share * part.astype(F32).reshape(AB, HD)
    result = (summed / (shares[0] + shares[1] + shares[2])).astype(BF16)
    for h in range(PEERS):
        out[:, h * HD : (h + 1) * HD] = result[h * AT : (h + 1) * AT]


IN_VMEM = pl.BlockSpec(memory_space=pltpu.VMEM)
IN_PLACE = pl.BlockSpec(memory_space=pltpu.HBM)
IN_SMEM = pl.BlockSpec(memory_space=pltpu.SMEM)


def cost(rows_, keys_, moved):
    return pl.CostEstimate(
        flops=4 * rows_ * keys_ * HD, bytes_accessed=moved, transcendentals=rows_ * keys_
    )


def scratch(keys_):
    return [
        pltpu.VMEM((keys_ - VB, HD), BF16),
        pltpu.VMEM((keys_, 2 * HD), BF16),
        pltpu.VMEM((2, STEP, keys_), F32),
    ]


def swap(block, first):
    pairs_ = [(i, i + 1) for i in range(first, BLOCKS - 1, 2)]
    return lax.ppermute(block, "seq", pairs_ + [(j, i) for i, j in pairs_])


def on_device(video_qkv, audio_qkv, pairs):
    params = pltpu.CompilerParams(vmem_limit_bytes=VMEM_LIMIT)
    pack_params = pltpu.CompilerParams(vmem_limit_bytes=PACK_LIMIT)

    cuts = 4
    packed_video = pl.pallas_call(
        pack_kernel,
        out_shape=jax.ShapeDtypeStruct((PEERS, 3 * VT, HD), BF16),
        in_specs=[IN_PLACE],
        out_specs=IN_VMEM,
        scratch_shapes=[
            pltpu.VMEM((cuts, 3, VT // cuts, PEERS * HD), BF16),
            pltpu.SemaphoreType.DMA((cuts,)),
        ],
        compiler_params=pack_params,
        cost_estimate=pl.CostEstimate(flops=0, bytes_accessed=4 << 20, transcendentals=0),
        name="pack_video",
    )(video_qkv.transpose(1, 0, 2))

    def exchanged(block):
        return lax.all_to_all(block, "head", split_axis=0, concat_axis=0, tiled=True)

    turned = audio_qkv.reshape(AT, 3, PEERS, HD).transpose(2, 1, 0, 3)
    own_audio = exchanged(turned.reshape(PEERS, 3 * AT, HD))
    own = exchanged(packed_video)
    far = swap(own_audio, 1)
    near = swap(own_audio, 0)
    parts = pl.pallas_call(
        lend_kernel,
        out_shape=jax.ShapeDtypeStruct((PEERS, 4, AT, HD), BF16),
        in_specs=[IN_VMEM] * 4,
        out_specs=IN_PLACE,
        scratch_shapes=scratch(VB + AB)
        + [
            pltpu.VMEM((3, AB, HD), F32),
            pltpu.VMEM((4, PEERS, AT, HD), BF16),
            pltpu.SemaphoreType.DMA((4,)),
        ],
        compiler_params=params,
        cost_estimate=cost(3 * AB, VB, 2 << 20),
        name="lend",
    )(own, own_audio, far, near)
    parts = exchanged(parts)
    out = pl.pallas_call(
        main_kernel,
        out_shape=jax.ShapeDtypeStruct((PEERS, VT, HD), BF16),
        in_specs=[IN_SMEM] + [IN_VMEM] * 4,
        out_specs=IN_PLACE,
        scratch_shapes=scratch(KEYS)
        + [pltpu.VMEM((PEERS, VT, HD), BF16), pltpu.SemaphoreType.DMA((VB // STEP,))],
        compiler_params=params,
        cost_estimate=cost(VB, KEYS, 3 << 20),
        name="attend",
    )(pairs, own, own_audio, far, near)
    back = exchanged(out)
    from_far = swap(parts[:, FAR_AT : MARKS_AT + 1], 1)
    from_near = swap(parts[:, MARKS_AT : NEAR_AT + 1], 0)
    audio_out = pl.pallas_call(
        merge_kernel,
        out_shape=jax.ShapeDtypeStruct((AT, PEERS * HD), BF16),
        in_specs=[IN_SMEM] + [IN_VMEM] * 3,
        out_specs=IN_VMEM,
        compiler_params=params,
        name="merge",
    )(pairs, parts, from_far, from_near)
    video_out = pl.pallas_call(
        unpack_kernel,
        out_shape=jax.ShapeDtypeStruct((VT, PEERS * HD), BF16),
        in_specs=[IN_VMEM],
        out_specs=IN_PLACE,
        scratch_shapes=[
            pltpu.VMEM((4, VT // 4, PEERS * HD), BF16),
            pltpu.SemaphoreType.DMA((4,)),
        ],
        compiler_params=params,
        name="unpack",
    )(back)
    return video_out, audio_out


def solution(mesh):
    return jax.shard_map(
        on_device,
        mesh=mesh,
        in_specs=(P(("seq", "head"), None, None), P(("seq", "head"), None, None), P()),
        out_specs=(P(("seq", "head"), None), P(("seq", "head"), None)),
        check_vma=False,
    )
```
